32 devices in a mesh: blk: 8 (over z, core), head: 4 (over y, x).
Axes of the slice: x: 2, y: 2, z: 4, core: 2. Of those that a mesh axis runs over, the one named last changes fastest.
Arguments:
- queries: bfloat16 [2048, 8192], P('blk', 'head'), may hold values from -4 to 10
- context_keys: bfloat16 [8192, 1024], P('blk', 'head'), may hold values from -4 to 7
- context_values: bfloat16 [8192, 1024], P('blk', 'head'), may hold values from -6 to 6
- response_keys: bfloat16 [2048, 1024], P('blk', 'head'), may hold values from -4 to 7
- response_values: bfloat16 [2048, 1024], P('blk', 'head'), may hold values from -6 to 6
- out_weight: bfloat16 [8192, 8192], P('head', 'blk'), may hold values from -0.09375 to 0.09375
- query_docs: int32 [16], replicated, may hold values from 0 to 2
- block_docs: int32 [64], replicated, may hold values from 0 to 2
- visits: int32 [16, 4, 8], replicated, may hold values 0 or 1
Outputs:
- mixed: bfloat16 [2048, 8192], P('blk', 'head')
The draws below stay inside these ranges and needn't reach their ends.
All inputs are finite; a program needn't handle non-finite values.
Results may differ from the reference program's by a relative error of at most 0.0165.
Values may be sent and summed in bfloat16 or wider, within the bound.
A program may use at most 128 MiB of HBM per device.

```python
import jax
import jax.numpy as jnp
from jax import lax

D = 8192
HQ = 64
KVH = 8
HD = 128
BLOCK = 128
HOPS = 3
DOCS = 3
TOK_DEV = 256
CTX_DEV = 1024
TOKENS = 2048
CTX = 8192
QBLOCKS = 16
CBLOCKS = 64
KVB = 8
N_BLK = 8


def draw_queries(key, part):
    values = jnp.clip(jax.random.normal(key, (TOKENS, HQ * HD), jnp.float32), -4.0, 4.0)
    return values.astype(jnp.bfloat16)


def draw_context_keys(key, part):
    values = jnp.clip(jax.random.normal(key, (CTX, KVH * HD), jnp.float32), -4.0, 4.0)
    return values.astype(jnp.bfloat16)


def draw_response_keys(key, part):
    values = jnp.clip(jax.random.normal(jax.random.fold_in(key, 11), (TOKENS, KVH * HD), jnp.float32), -4.0, 4.0)
    return values.astype(jnp.bfloat16)


def plant(entries, stream_key, least, largest):
    longest = entries.shape.index(max(entries.shape))
    spots = []
    for shift in (0, 1):
        where = [jax.random.randint(jax.random.fold_in(stream_key, axis), (), 0, length) for axis, length in enumerate(entries.shape)]
        where[longest] = (where[longest] + shift) % entries.shape[longest]
        spots.append(tuple(where))
    return entries.at[spots[0]].set(least).at[spots[1]].set(largest)


def spiked(values, own_key, source, target, blocks, factor):
    owner, partner = [(jnp.arange(values.shape[position]) // (values.shape[position] // blocks)).reshape([-1 if axis == position else 1 for axis in range(values.ndim)]) for position in (source, target)]
    chosen = jax.random.permutation(own_key, blocks)[partner]
    strong = (owner == chosen) | (owner == (partner + blocks // 2) % blocks)
    return jnp.where(strong, factor * values, values)


def shard_levels(key, shape, pieces, smallest, largest):
    level = 1.0
    for position, shards_of in pieces:
        heights = jax.random.uniform(jax.random.fold_in(jax.random.fold_in(key, 6), position), (shards_of,), jnp.float32, smallest / len(pieces), largest / len(pieces))
        level = level * jnp.repeat(jnp.exp(heights), shape[position] // shards_of).reshape((-1,) + (1,) * (len(shape) - 1 - position))
    return level


def centred(key, dims, deviation, bound, split=(), kind=jnp.bfloat16):
    array = jax.random.normal(key, dims, jnp.float32) * deviation
    if len(split) > 0:
        array = shard_levels(key, dims, split, -0.22, 0.18) * array
    return jnp.clip(array, min=-bound, max=bound).astype(kind)


def bell_draw_with(rng, extent, deviation, bound, cuts, heavy, kind=jnp.bfloat16):
    entries = deviation * jax.random.normal(rng, extent, jnp.float32)
    if cuts:
        entries = entries * shard_levels(rng, extent, cuts, -0.22, 0.18)
    return jnp.clip(spiked(entries, jax.random.fold_in(rng, 3), *heavy), -bound, bound).astype(kind)


def setup_inputs(seed: int = 0) -> dict:
    streams_of = jax.random.split(jax.random.key(seed), 10)
    return {
        "queries": draw_queries(jax.random.fold_in(streams_of[9], 71), 0),
        "context_keys": draw_context_keys(jax.random.fold_in(streams_of[9], 71), 0),
        "context_values": centred(streams_of[2], (CTX, KVH * HD), 1.0, 6.0, ((0, 8), (1, 4))),
        "response_keys": draw_response_keys(jax.random.fold_in(streams_of[9], 71), 0),
        "response_values": centred(streams_of[4], (TOKENS, KVH * HD), 1.0, 6.0, ((0, 8), (1, 4))),
        "out_weight": bell_draw_with(streams_of[5], (HQ * HD, D), (HQ * HD) ** -0.5, 0.09375, ((0, 4), (1, 8)), (0, 1, 8, 2.0)),
        "query_docs": plant(jax.random.randint(streams_of[6], (QBLOCKS,), 0, DOCS), jax.random.fold_in(streams_of[6], 1), 0, DOCS - 1).astype(jnp.int32),
        "block_docs": plant(jax.random.randint(streams_of[7], (CBLOCKS,), 0, DOCS), jax.random.fold_in(streams_of[7], 1), 0, DOCS - 1).astype(jnp.int32),
        "visits": plant((jax.random.randint(streams_of[8], (QBLOCKS, HOPS + 1, KVB), 0, 2) < 1).astype(jnp.int32), jax.random.fold_in(streams_of[8], 1), 0, 1),
    }


def reference(queries, context_keys, context_values, response_keys, response_values, out_weight, query_docs, block_docs, visits):
    per_group = HQ // KVH
    softmax_scale = HD ** -0.5
    query_heads = queries.reshape(N_BLK, TOK_DEV, KVH, per_group, HD)
    key_shards = context_keys.reshape(N_BLK, CTX_DEV, KVH, HD)
    value_shards = context_values.reshape(N_BLK, CTX_DEV, KVH, HD)
    own_keys = response_keys.reshape(N_BLK, TOK_DEV, KVH, HD)
    own_values = response_values.reshape(N_BLK, TOK_DEV, KVH, HD)
    query_doc = query_docs.reshape(N_BLK, TOK_DEV // BLOCK)
    block_doc = block_docs.reshape(N_BLK, KVB)
    visited = visits.reshape(N_BLK, TOK_DEV // BLOCK, HOPS + 1, KVB)
    row_block = (jnp.arange(TOK_DEV) // BLOCK).astype(jnp.int32)
    key_block = (jnp.arange(CTX_DEV) // BLOCK).astype(jnp.int32)
    positions = jnp.arange(TOK_DEV)
    causal = positions[:, None] >= positions[None, :]

    def one_shard(anchor):
        holders = ((anchor + jnp.arange(HOPS + 1)) % N_BLK).astype(jnp.int32)
        all_keys = jnp.concatenate([key_shards[holders].reshape((HOPS + 1) * CTX_DEV, KVH, HD), own_keys[anchor]], axis=0)
        all_values = jnp.concatenate([value_shards[holders].reshape((HOPS + 1) * CTX_DEV, KVH, HD), own_values[anchor]], axis=0)
        visit_rows = visited[anchor][row_block] == 1
        doc_match = block_doc[holders][None, :, :] == query_doc[anchor][row_block][:, None, None]
        block_allow = visit_rows & doc_match
        context_allow = block_allow[:, :, key_block].reshape(TOK_DEV, (HOPS + 1) * CTX_DEV)
        allowed = jnp.concatenate([context_allow, causal], axis=1)

        def one_head(kv_head):
            query_part = query_heads[anchor][:, kv_head].astype(jnp.float32)
            key_part = all_keys[:, kv_head].astype(jnp.float32)
            value_part = all_values[:, kv_head].astype(jnp.float32)
            scores = jnp.einsum('tjd,sd->tjs', query_part, key_part) * softmax_scale
            scores = jnp.where(allowed[:, None, :], scores, -jnp.inf)
            highest = jnp.max(scores, axis=-1, keepdims=True)
            weights = jnp.exp(scores - highest)
            weight_sum = jnp.sum(weights, axis=-1)
            rounded = lax.optimization_barrier(weights.astype(jnp.bfloat16)).astype(jnp.float32)
            summed = jnp.einsum('tjs,sd->tjd', rounded, value_part)
            return summed / weight_sum[:, :, None]

        heads_out = lax.map(one_head, jnp.arange(KVH))
        return jnp.transpose(heads_out, (1, 0, 2, 3)).reshape(TOK_DEV, HQ * HD).astype(jnp.bfloat16)

    attended = lax.map(one_shard, jnp.arange(N_BLK)).reshape(TOKENS, HQ * HD)
    return jnp.dot(attended, out_weight, preferred_element_type=jnp.float32).astype(jnp.bfloat16)
```

```python
import functools

import jax
import jax.numpy as jnp
from jax import lax
from jax.experimental import pallas as pl
from jax.experimental.pallas import tpu as pltpu
from jax.sharding import PartitionSpec as P

HD = 128
BLOCK = 128
HOPS = 3
PIECES = 4
HALVES = 2
MESH = pl.DeviceIdType.MESH
VMEM_BYTES = 56 * 1024 * 1024
LOG2E = 1.4426950408889634


def collect(devices, k_ref, v_ref, k_all, v_all, own_sem, send_sem, recv_sem):
    me, row = lax.axis_index("blk"), lax.axis_index("head")
    left, right = lax.rem(me + devices - 1, devices), lax.rem(me + 1, devices)
    barrier = pltpu.get_barrier_semaphore()
    for other in (left, right):
        pl.semaphore_signal(barrier, inc=1, device_id=(other, row), device_id_type=MESH)
    pl.semaphore_wait(barrier, 2)
    size = k_ref.shape[0] // PIECES

    def hop(step, which, piece):
        source, store = ((k_ref, k_all), (v_ref, v_all))[which]
        rows = pl.ds(piece * size, size)
        return pltpu.make_async_remote_copy(
            src_ref=source.at[rows] if step == 0 else store.at[step, rows],
            dst_ref=store.at[step + 1, rows],
            send_sem=send_sem.at[step, which, piece],
            recv_sem=recv_sem.at[step, which, piece],
            device_id=(left, row),
            device_id_type=MESH,
        )

    parts = [(which, piece) for piece in range(PIECES) for which in range(2)]
    for part in parts:
        hop(0, *part).start()
    own = [
        pltpu.make_async_copy(k_ref, k_all.at[0], own_sem.at[0]),
        pltpu.make_async_copy(v_ref, v_all.at[0], own_sem.at[1]),
    ]
    for copy in own:
        copy.start()
    for step in range(1, HOPS):
        for part in parts:
            hop(step - 1, *part).wait_recv()
            hop(step, *part).start()
    for part in parts:
        hop(HOPS - 1, *part).wait_recv()
    for step in range(HOPS):
        for part in parts:
            hop(step, *part).wait_send()
    for copy in own:
        copy.wait()


def attend(
    devices, kvb, qdoc_ref, bdoc_ref, visit_ref, q_ref, k_ref, v_ref, rk_ref, rv_ref, o_ref,
    chosen, top, total, acc
):
    me = lax.axis_index("blk")
    block_here = pl.program_id(1)
    row_blocks = pl.num_programs(1)
    query_block = me * row_blocks + block_here
    doc = qdoc_ref[query_block]
    slots = (HOPS + 1) * kvb

    def choose(slot, count):
        step = lax.div(slot, kvb)
        holder = lax.rem(me + step, devices)
        seen = visit_ref[query_block * slots + slot] == 1
        same = bdoc_ref[holder * kvb + lax.rem(slot, kvb)] == doc
        chosen[count] = slot
        return count + jnp.where(seen & same, 1, 0)

    chosen[0] = 0
    count = lax.fori_loop(0, slots, choose, 0)
    group = q_ref.shape[1] // HD
    rows = group * BLOCK
    queries = jnp.concatenate([q_ref[:, j * HD : (j + 1) * HD] for j in range(group)], axis=0)
    scale = HD**-0.5 * LOG2E

    def scored(keys):
        return lax.dot_general(
            queries, keys, (((1,), (1,)), ((), ())), preferred_element_type=jnp.float32
        ) * scale

    scores = scored(rk_ref[...])
    place = lax.rem(lax.broadcasted_iota(jnp.int32, scores.shape, 0), BLOCK) + block_here * BLOCK
    scores = jnp.where(lax.broadcasted_iota(jnp.int32, scores.shape, 1) <= place, scores, -jnp.inf)
    first = jnp.max(scores, axis=1, keepdims=True)
    weights = jnp.exp2(scores - first)
    top[...] = first
    total[...] = jnp.sum(weights, axis=1, keepdims=True)
    acc[...] = jnp.dot(
        weights.astype(jnp.bfloat16), rv_ref[...], preferred_element_type=jnp.float32
    )

    def pair(i, carry):
        one = pl.ds(pl.multiple_of(chosen[2 * i] * BLOCK, BLOCK), BLOCK)
        full = 2 * i + 1 < count
        other = jnp.where(full, chosen[2 * i + 1], chosen[2 * i])
        two = pl.ds(pl.multiple_of(other * BLOCK, BLOCK), BLOCK)
        scores = scored(jnp.concatenate([k_ref[one, :], k_ref[two, :]], axis=0))
        limit = jnp.where(full, 2 * BLOCK, BLOCK)
        scores = jnp.where(
            lax.broadcasted_iota(jnp.int32, scores.shape, 1) < limit, scores, -jnp.inf
        )
        before = top[...]
        now = jnp.maximum(before, jnp.max(scores, axis=1, keepdims=True))
        weights = jnp.exp2(scores - now)
        factor = jnp.exp2(before - now)
        top[...] = now
        total[...] = total[...] * factor + jnp.sum(weights, axis=1, keepdims=True)
        values = jnp.concatenate([v_ref[one, :], v_ref[two, :]], axis=0)
        acc[...] = acc[...] * factor + jnp.dot(
            weights.astype(jnp.bfloat16), values, preferred_element_type=jnp.float32
        )
        return carry

    lax.fori_loop(0, lax.div(count + 1, 2), pair, 0)
    result = (acc[...] / total[...]).astype(jnp.bfloat16)
    for j in range(group):
        o_ref[:, j * HD : (j + 1) * HD] = result[j * BLOCK : (j + 1) * BLOCK, :]


def project(
    members, a_ref, w_ref, out_ref, w_pair, blocks, parts, inbox, sums,
    w_sem, a_down, a_up, a_recv, part_send, part_recv, sum_send, sum_recv
):
    me, head = lax.axis_index("blk"), lax.axis_index("head")
    spot, core = lax.div(me, 2), lax.rem(me, 2)
    half_rows = a_ref.shape[0] // HALVES
    piece = half_rows // members
    width = w_ref.shape[1]

    barrier = pltpu.get_barrier_semaphore()
    for p in range(members):
        for h in range(members):
            @pl.when((p != spot) | (h != head))
            def _():
                pl.semaphore_signal(
                    barrier, inc=1, device_id=(2 * p + core, h), device_id_type=MESH
                )
    pl.semaphore_signal(barrier, inc=1, device_id=(2 * spot + 1 - core, head), device_id_type=MESH)
    pl.semaphore_wait(barrier, members * members)

    def along(source, half, down):
        rows = pl.ds(half * half_rows, half_rows)
        return functools.partial(
            pltpu.make_async_remote_copy,
            dst_ref=blocks.at[source, rows],
            send_sem=(a_down if down else a_up).at[source, half],
            recv_sem=a_recv.at[source, half],
            device_id=(2 * (spot - 1 if down else spot + 1) + core, head),
            device_id_type=MESH,
        )

    def pass_on(source, half, own, down, act):
        rows = pl.ds(half * half_rows, half_rows)
        origin = a_ref.at[rows] if own else blocks.at[source, rows]

        @pl.when(spot > 0 if down else spot < members - 1)
        def _():
            act(along(source, half, down)(src_ref=origin))

    start = lambda copy: copy.start()
    finish = lambda copy: copy.wait_send()
    for half in range(HALVES):
        pass_on(spot, half, True, True, start)
        pass_on(spot, half, True, False, start)
    swap = pltpu.make_async_remote_copy(
        src_ref=w_ref,
        dst_ref=w_pair,
        send_sem=w_sem.at[0],
        recv_sem=w_sem.at[1],
        device_id=(2 * spot + 1 - core, head),
        device_id_type=MESH,
    )
    swap.start()

    def part_copy(source, half, k):
        peer = lax.rem(head + k, members)
        return pltpu.make_async_remote_copy(
            src_ref=parts.at[source, half, pl.ds(pl.multiple_of(peer * piece, piece), piece)],
            dst_ref=inbox.at[source, half, k - 1],
            send_sem=part_send.at[source, half, k - 1],
            recv_sem=part_recv.at[source, half, k - 1],
            device_id=(me, peer),
            device_id_type=MESH,
        )

    def sum_copy(source, half):
        rows = pl.ds(pl.multiple_of(half * half_rows + head * piece, piece), piece)
        return pltpu.make_async_remote_copy(
            src_ref=sums.at[source, half],
            dst_ref=out_ref.at[rows],
            send_sem=sum_send.at[source, half],
            recv_sem=sum_recv.at[half, head],
            device_id=(2 * source + core, spot),
            device_id_type=MESH,
        )

    def multiply(source, half, own):
        rows = pl.ds(half * half_rows, half_rows)
        left = a_ref.at[rows] if own else blocks.at[source, rows]
        tile = min(width, 512)
        for right, place in ((w_ref, core), (w_pair, 1 - core)):
            if own and half == 0 and right is w_pair:
                swap.wait_recv()

            @pl.loop(0, width // tile)
            def _(t):
                at = pl.multiple_of(t * tile, tile)
                to = pl.multiple_of(place * width + t * tile, tile)
                parts[source, half, :, pl.ds(to, tile)] = jnp.dot(
                    left[...], right[:, pl.ds(at, tile)], preferred_element_type=jnp.float32
                ).astype(jnp.bfloat16)

    def spread(source, half, own, from_above):
        if not own:
            along(source, half, from_above)(src_ref=blocks.at[source, pl.ds(half * half_rows, half_rows)]).wait_recv()
            pass_on(source, half, False, from_above, start)
        multiply(source, half, own)
        for k in range(1, members):
            part_copy(source, half, k).start()

    def reduce(source, half):
        mine = pl.ds(pl.multiple_of(head * piece, piece), piece)
        value = parts[source, half, mine, :].astype(jnp.float32)
        for k in range(1, members):
            part_copy(source, half, k).wait_recv()
            value += inbox[source, half, k - 1].astype(jnp.float32)
        here = (source == spot) & (head == spot)
        rows = pl.ds(pl.multiple_of(half * half_rows + head * piece, piece), piece)

        @pl.when(here)
        def _():
            out_ref[rows, :] = value.astype(jnp.bfloat16)

        @pl.when(jnp.logical_not(here))
        def _():
            sums[source, half] = value.astype(jnp.bfloat16)
            sum_copy(source, half).start()

    events = [(spot, half, True, False, None) for half in range(HALVES)]
    for step in range(1, members):
        for half in range(HALVES):
            events.append((spot + step, half, False, True, spot + step < members))
            events.append((spot - step, half, False, False, spot - step >= 0))

    def run(valid, work):
        if valid is None:
            work()
        else:
            pl.when(valid)(work)

    lag = 2
    for i in range(len(events) + lag):
        if i < len(events):
            source, half, own, from_above, valid = events[i]
            run(valid, functools.partial(spread, source, half, own, from_above))
        if i >= lag:
            source, half, _, _, valid = events[i - lag]
            run(valid, functools.partial(reduce, source, half))

    for source, half, own, from_above, valid in events:
        def done(source=source, half=half, own=own, from_above=from_above):
            if own:
                pass_on(source, half, True, True, finish)
                pass_on(source, half, True, False, finish)
            else:
                pass_on(source, half, False, from_above, finish)
            for k in range(1, members):
                part_copy(source, half, k).wait_send()

            @pl.when((source != spot) | (head != spot))
            def _():
                sum_copy(source, half).wait_send()

        run(valid, done)
    swap.wait_send()
    for half in range(HALVES):
        for k in range(members):
            rows = pl.ds(half * half_rows + k * piece, piece)

            @pl.when((k != head) | (spot != head))
            def _():
                pltpu.make_async_remote_copy(
                    src_ref=sums.at[0, 0],
                    dst_ref=out_ref.at[rows],
                    send_sem=sum_send.at[0, 0],
                    recv_sem=sum_recv.at[half, k],
                    device_id=(2 * head + core, k),
                    device_id_type=MESH,
                ).wait_recv()


def shards(
    queries,
    context_keys,
    context_values,
    response_keys,
    response_values,
    out_weight,
    query_docs,
    block_docs,
    visits,
):
    devices, members = lax.axis_size("blk"), lax.axis_size("head")
    assert devices == 2 * members
    rows_here, lanes = queries.shape
    key_rows, key_lanes = context_keys.shape
    heads_here = key_lanes // HD
    group = lanes // heads_here
    kvb = key_rows // BLOCK
    slots = HOPS + 1
    dma = pltpu.SemaphoreType.DMA
    anywhere = pl.BlockSpec(memory_space=pl.ANY)
    in_vmem = pl.BlockSpec(memory_space=pltpu.VMEM)
    in_smem = pl.BlockSpec(memory_space=pltpu.SMEM)

    store = jax.ShapeDtypeStruct((slots, key_rows, key_lanes), jnp.bfloat16)
    all_keys, all_values = pl.pallas_call(
        functools.partial(collect, devices),
        out_shape=(store, store),
        in_specs=[anywhere] * 2,
        out_specs=(anywhere, anywhere),
        scratch_shapes=[dma((2,)), dma((HOPS, 2, PIECES)), dma((HOPS, 2, PIECES))],
        compiler_params=pltpu.CompilerParams(
            collective_id=0, has_side_effects=True, vmem_limit_bytes=VMEM_BYTES
        ),
        name="collect",
    )(context_keys, context_values)

    whole = lambda: pl.BlockSpec((slots * key_rows, HD), lambda g, b: (0, g))
    own = lambda: pl.BlockSpec((rows_here, HD), lambda g, b: (0, g))
    attended = pl.pallas_call(
        functools.partial(attend, devices, kvb),
        grid=(heads_here, rows_here // BLOCK),
        out_shape=jax.ShapeDtypeStruct((rows_here, lanes), jnp.bfloat16),
        in_specs=[in_smem] * 3
        + [pl.BlockSpec((BLOCK, group), lambda g, b: (b, g)), whole(), whole(), own(), own()],
        out_specs=pl.BlockSpec((BLOCK, group), lambda g, b: (b, g)),
        scratch_shapes=[
            pltpu.SMEM((slots * kvb + 1,), jnp.int32),
            pltpu.VMEM((group // HD * BLOCK, 1), jnp.float32),
            pltpu.VMEM((group // HD * BLOCK, 1), jnp.float32),
            pltpu.VMEM((group // HD * BLOCK, HD), jnp.float32),
        ],
        compiler_params=pltpu.CompilerParams(vmem_limit_bytes=VMEM_BYTES),
        name="attend",
    )(
        query_docs,
        block_docs,
        visits.reshape(-1),
        queries,
        all_keys.reshape(slots * key_rows, key_lanes),
        all_values.reshape(slots * key_rows, key_lanes),
        response_keys,
        response_values,
    )

    depth, width = out_weight.shape
    half_rows = rows_here // HALVES
    piece = half_rows // members
    half = jnp.bfloat16
    return pl.pallas_call(
        functools.partial(project, members),
        out_shape=jax.ShapeDtypeStruct((rows_here, 2 * width), half),
        in_specs=[in_vmem] * 2,
        out_specs=in_vmem,
        scratch_shapes=[
            pltpu.VMEM((depth, width), half),
            pltpu.VMEM((members, rows_here, depth), half),
            pltpu.VMEM((members, HALVES, half_rows, 2 * width), half),
            pltpu.VMEM((members, HALVES, members - 1, piece, 2 * width), half),
            pltpu.VMEM((members, HALVES, piece, 2 * width), half),
            dma((2,)),
            dma((members, HALVES)),
            dma((members, HALVES)),
            dma((members, HALVES)),
            dma((members, HALVES, members - 1)),
            dma((members, HALVES, members - 1)),
            dma((members, HALVES)),
            dma((HALVES, members)),
        ],
        compiler_params=pltpu.CompilerParams(
            collective_id=1, has_side_effects=True, vmem_limit_bytes=VMEM_BYTES
        ),
        name="project",
    )(attended, out_weight)


def solution(mesh):
    in_specs = (
        P("blk", "head"),
        P("blk", "head"),
        P("blk", "head"),
        P("blk", "head"),
        P("blk", "head"),
        P("head", "blk"),
        P(),
        P(),
        P(),
    )
    out_specs = P("blk", "head")
    return jax.shard_map(shards, mesh=mesh, in_specs=in_specs, out_specs=out_specs, check_vma=False)
```

```python
import functools

import jax
import jax.numpy as jnp
from jax import lax
from jax.experimental import pallas as pl
from jax.experimental.pallas import tpu as pltpu
from jax.sharding import PartitionSpec as P

HD = 128
BLOCK = 128
HOPS = 3
PIECES = 4
HALVES = 2
MESH = pl.DeviceIdType.MESH
VMEM_BYTES = 56 * 1024 * 1024
LOG2E = 1.4426950408889634


def collect(devices, k_ref, v_ref, k_all, v_all, own_sem, send_sem, recv_sem):
    me, row = lax.axis_index("blk"), lax.axis_index("head")
    left, right = lax.rem(me + devices - 1, devices), lax.rem(me + 1, devices)
    barrier = pltpu.get_barrier_semaphore()
    for other in (left, right):
        pl.semaphore_signal(barrier, inc=1, device_id=(other, row), device_id_type=MESH)
    pl.semaphore_wait(barrier, 2)
    size = k_ref.shape[0] // PIECES

    def hop(step, which, piece):
        source, store = ((k_ref, k_all), (v_ref, v_all))[which]
        rows = pl.ds(piece * size, size)
        return pltpu.make_async_remote_copy(
            src_ref=source.at[rows] if step == 0 else store.at[step, rows],
            dst_ref=store.at[step + 1, rows],
            send_sem=send_sem.at[step, which, piece],
            recv_sem=recv_sem.at[step, which, piece],
            device_id=(left, row),
            device_id_type=MESH,
        )

    parts = [(which, piece) for piece in range(PIECES) for which in range(2)]
    for part in parts:
        hop(0, *part).start()
    own = [
        pltpu.make_async_copy(k_ref, k_all.at[0], own_sem.at[0]),
        pltpu.make_async_copy(v_ref, v_all.at[0], own_sem.at[1]),
    ]
    for copy in own:
        copy.start()
    for step in range(1, HOPS):
        for part in parts:
            hop(step - 1, *part).wait_recv()
            hop(step, *part).start()
    for part in parts:
        hop(HOPS - 1, *part).wait_recv()
    for step in range(HOPS):
        for part in parts:
            hop(step, *part).wait_send()
    for copy in own:
        copy.wait()


def attend(
    devices, kvb, qdoc_ref, bdoc_ref, visit_ref, q_ref, k_ref, v_ref, rk_ref, rv_ref, o_ref,
    chosen, turned, top, total, acc
):
    me = lax.axis_index("blk")
    block_here = pl.program_id(1)
    row_blocks = pl.num_programs(1)
    query_block = me * row_blocks + block_here
    doc = qdoc_ref[query_block]
    slots = (HOPS + 1) * kvb

    def choose(slot, count):
        step = lax.div(slot, kvb)
        holder = lax.rem(me + step, devices)
        seen = visit_ref[query_block * slots + slot] == 1
        same = bdoc_ref[holder * kvb + lax.rem(slot, kvb)] == doc
        chosen[count] = slot
        return count + jnp.where(seen & same, 1, 0)

    chosen[0] = 0
    count = lax.fori_loop(0, slots, choose, 0)
    group = q_ref.shape[1] // HD
    for j in range(group):
        turned[:, j * BLOCK : (j + 1) * BLOCK] = q_ref[:, j * HD : (j + 1) * HD].T
    scale = HD**-0.5 * LOG2E

    def scored(keys):
        return jnp.dot(keys, turned[...], preferred_element_type=jnp.float32) * scale

    def weighted(values, weights):
        return lax.dot_general(
            values,
            weights.astype(jnp.bfloat16),
            (((0,), (0,)), ((), ())),
            preferred_element_type=jnp.float32,
        )

    scores = scored(rk_ref[...])
    place = lax.rem(lax.broadcasted_iota(jnp.int32, scores.shape, 1), BLOCK) + block_here * BLOCK
    scores = jnp.where(lax.broadcasted_iota(jnp.int32, scores.shape, 0) <= place, scores, -jnp.inf)
    first = jnp.max(scores, axis=0, keepdims=True)
    weights = jnp.exp2(scores - first)
    top[...] = first
    total[...] = jnp.sum(weights, axis=0, keepdims=True)
    acc[...] = weighted(rv_ref[...], weights)

    def add(keys, values):
        scores = scored(keys)
        before = top[...]
        now = jnp.maximum(before, jnp.max(scores, axis=0, keepdims=True))
        weights = jnp.exp2(scores - now)
        factor = jnp.exp2(before - now)
        top[...] = now
        total[...] = total[...] * factor + jnp.sum(weights, axis=0, keepdims=True)
        acc[...] = acc[...] * factor + weighted(values, weights)

    def rows_of(i):
        return pl.ds(pl.multiple_of(chosen[i] * BLOCK, BLOCK), BLOCK)

    def pair(i, carry):
        one, two = rows_of(2 * i), rows_of(2 * i + 1)
        add(
            jnp.concatenate([k_ref[one, :], k_ref[two, :]], axis=0),
            jnp.concatenate([v_ref[one, :], v_ref[two, :]], axis=0),
        )
        return carry

    lax.fori_loop(0, lax.div(count, 2), pair, 0)

    @pl.when(lax.rem(count, 2) == 1)
    def _():
        last = rows_of(count - 1)
        add(k_ref[last, :], v_ref[last, :])

    result = (acc[...] / total[...]).astype(jnp.bfloat16)
    for j in range(group):
        o_ref[:, j * HD : (j + 1) * HD] = result[:, j * BLOCK : (j + 1) * BLOCK].T


def project(
    members, a_ref, w_ref, out_ref, w_pair, blocks, parts, inbox, sums,
    w_sem, a_down, a_up, a_recv, part_send, part_recv, sum_send, sum_recv
):
    me, head = lax.axis_index("blk"), lax.axis_index("head")
    spot, core = lax.div(me, 2), lax.rem(me, 2)
    half_rows = a_ref.shape[0] // HALVES
    piece = half_rows // members
    width = w_ref.shape[1]

    barrier = pltpu.get_barrier_semaphore()
    for p in range(members):
        for h in range(members):
            @pl.when((p != spot) | (h != head))
            def _():
                pl.semaphore_signal(
                    barrier, inc=1, device_id=(2 * p + core, h), device_id_type=MESH
                )
    pl.semaphore_signal(barrier, inc=1, device_id=(2 * spot + 1 - core, head), device_id_type=MESH)
    pl.semaphore_wait(barrier, members * members)

    def along(source, half, down):
        rows = pl.ds(half * half_rows, half_rows)
        return functools.partial(
            pltpu.make_async_remote_copy,
            dst_ref=blocks.at[source, rows],
            send_sem=(a_down if down else a_up).at[source, half],
            recv_sem=a_recv.at[source, half],
            device_id=(2 * (spot - 1 if down else spot + 1) + core, head),
            device_id_type=MESH,
        )

    def pass_on(source, half, own, down, act):
        rows = pl.ds(half * half_rows, half_rows)
        origin = a_ref.at[rows] if own else blocks.at[source, rows]

        @pl.when(spot > 0 if down else spot < members - 1)
        def _():
            act(along(source, half, down)(src_ref=origin))

    start = lambda copy: copy.start()
    finish = lambda copy: copy.wait_send()
    for half in range(HALVES):
        pass_on(spot, half, True, True, start)
        pass_on(spot, half, True, False, start)
    swap = pltpu.make_async_remote_copy(
        src_ref=w_ref,
        dst_ref=w_pair,
        send_sem=w_sem.at[0],
        recv_sem=w_sem.at[1],
        device_id=(2 * spot + 1 - core, head),
        device_id_type=MESH,
    )
    swap.start()

    def part_copy(source, half, k):
        peer = lax.rem(head + k, members)
        return pltpu.make_async_remote_copy(
            src_ref=parts.at[source, half, pl.ds(pl.multiple_of(peer * piece, piece), piece)],
            dst_ref=inbox.at[source, half, k - 1],
            send_sem=part_send.at[source, half, k - 1],
            recv_sem=part_recv.at[source, half, k - 1],
            device_id=(me, peer),
            device_id_type=MESH,
        )

    def sum_copy(source, half):
        rows = pl.ds(pl.multiple_of(half * half_rows + head * piece, piece), piece)
        return pltpu.make_async_remote_copy(
            src_ref=sums.at[source, half],
            dst_ref=out_ref.at[rows],
            send_sem=sum_send.at[source, half],
            recv_sem=sum_recv.at[half, head],
            device_id=(2 * source + core, spot),
            device_id_type=MESH,
        )

    def multiply(source, half, own):
        rows = pl.ds(half * half_rows, half_rows)
        left = a_ref.at[rows] if own else blocks.at[source, rows]
        tile = min(width, 512)
        for right, place in ((w_ref, core), (w_pair, 1 - core)):
            if own and half == 0 and right is w_pair:
                swap.wait_recv()

            @pl.loop(0, width // tile)
            def _(t):
                at = pl.multiple_of(t * tile, tile)
                to = pl.multiple_of(place * width + t * tile, tile)
                parts[source, half, :, pl.ds(to, tile)] = jnp.dot(
                    left[...], right[:, pl.ds(at, tile)], preferred_element_type=jnp.float32
                ).astype(jnp.bfloat16)

    def spread(source, half, own, from_above):
        if not own:
            along(source, half, from_above)(src_ref=blocks.at[source, pl.ds(half * half_rows, half_rows)]).wait_recv()
            pass_on(source, half, False, from_above, start)
        multiply(source, half, own)
        for k in range(1, members):
            part_copy(source, half, k).start()

    def reduce(source, half):
        mine = pl.ds(pl.multiple_of(head * piece, piece), piece)
        value = parts[source, half, mine, :].astype(jnp.float32)
        for k in range(1, members):
            part_copy(source, half, k).wait_recv()
            value += inbox[source, half, k - 1].astype(jnp.float32)
        here = (source == spot) & (head == spot)
        rows = pl.ds(pl.multiple_of(half * half_rows + head * piece, piece), piece)

        @pl.when(here)
        def _():
            out_ref[rows, :] = value.astype(jnp.bfloat16)

        @pl.when(jnp.logical_not(here))
        def _():
            sums[source, half] = value.astype(jnp.bfloat16)
            sum_copy(source, half).start()

    events = [(spot, half, True, False, None) for half in range(HALVES)]
    for step in range(1, members):
        for half in range(HALVES):
            events.append((spot + step, half, False, True, spot + step < members))
            events.append((spot - step, half, False, False, spot - step >= 0))

    def run(valid, work):
        if valid is None:
            work()
        else:
            pl.when(valid)(work)

    lag = 2
    for i in range(len(events) + lag):
        if i < len(events):
            source, half, own, from_above, valid = events[i]
            run(valid, functools.partial(spread, source, half, own, from_above))
        if i >= lag:
            source, half, _, _, valid = events[i - lag]
            run(valid, functools.partial(reduce, source, half))

    for source, half, own, from_above, valid in events:
        def done(source=source, half=half, own=own, from_above=from_above):
            if own:
                pass_on(source, half, True, True, finish)
                pass_on(source, half, True, False, finish)
            else:
                pass_on(source, half, False, from_above, finish)
            for k in range(1, members):
                part_copy(source, half, k).wait_send()

            @pl.when((source != spot) | (head != spot))
            def _():
                sum_copy(source, half).wait_send()

        run(valid, done)
    swap.wait_send()
    for half in range(HALVES):
        for k in range(members):
            rows = pl.ds(half * half_rows + k * piece, piece)

            @pl.when((k != head) | (spot != head))
            def _():
                pltpu.make_async_remote_copy(
                    src_ref=sums.at[0, 0],
                    dst_ref=out_ref.at[rows],
                    send_sem=sum_send.at[0, 0],
                    recv_sem=sum_recv.at[half, k],
                    device_id=(2 * head + core, k),
                    device_id_type=MESH,
                ).wait_recv()


def shards(
    queries,
    context_keys,
    context_values,
    response_keys,
    response_values,
    out_weight,
    query_docs,
    block_docs,
    visits,
):
    devices, members = lax.axis_size("blk"), lax.axis_size("head")
    assert devices == 2 * members
    rows_here, lanes = queries.shape
    key_rows, key_lanes = context_keys.shape
    heads_here = key_lanes // HD
    group = lanes // heads_here
    kvb = key_rows // BLOCK
    slots = HOPS + 1
    dma = pltpu.SemaphoreType.DMA
    anywhere = pl.BlockSpec(memory_space=pl.ANY)
    in_vmem = pl.BlockSpec(memory_space=pltpu.VMEM)
    in_smem = pl.BlockSpec(memory_space=pltpu.SMEM)

    store = jax.ShapeDtypeStruct((slots, key_rows, key_lanes), jnp.bfloat16)
    all_keys, all_values = pl.pallas_call(
        functools.partial(collect, devices),
        out_shape=(store, store),
        in_specs=[anywhere] * 2,
        out_specs=(anywhere, anywhere),
        scratch_shapes=[dma((2,)), dma((HOPS, 2, PIECES)), dma((HOPS, 2, PIECES))],
        compiler_params=pltpu.CompilerParams(
            collective_id=0, has_side_effects=True, vmem_limit_bytes=VMEM_BYTES
        ),
        name="collect",
    )(context_keys, context_values)

    whole = lambda: pl.BlockSpec((slots * key_rows, HD), lambda g, b: (0, g))
    own = lambda: pl.BlockSpec((rows_here, HD), lambda g, b: (0, g))
    attended = pl.pallas_call(
        functools.partial(attend, devices, kvb),
        grid=(heads_here, rows_here // BLOCK),
        out_shape=jax.ShapeDtypeStruct((rows_here, lanes), jnp.bfloat16),
        in_specs=[in_smem] * 3
        + [pl.BlockSpec((BLOCK, group), lambda g, b: (b, g)), whole(), whole(), own(), own()],
        out_specs=pl.BlockSpec((BLOCK, group), lambda g, b: (b, g)),
        scratch_shapes=[
            pltpu.SMEM((slots * kvb + 1,), jnp.int32),
            pltpu.VMEM((HD, group // HD * BLOCK), jnp.bfloat16),
            pltpu.VMEM((1, group // HD * BLOCK), jnp.float32),
            pltpu.VMEM((1, group // HD * BLOCK), jnp.float32),
            pltpu.VMEM((HD, group // HD * BLOCK), jnp.float32),
        ],
        compiler_params=pltpu.CompilerParams(vmem_limit_bytes=VMEM_BYTES),
        name="attend",
    )(
        query_docs,
        block_docs,
        visits.reshape(-1),
        queries,
        all_keys.reshape(slots * key_rows, key_lanes),
        all_values.reshape(slots * key_rows, key_lanes),
        response_keys,
        response_values,
    )

    depth, width = out_weight.shape
    half_rows = rows_here // HALVES
    piece = half_rows // members
    half = jnp.bfloat16
    return pl.pallas_call(
        functools.partial(project, members),
        out_shape=jax.ShapeDtypeStruct((rows_here, 2 * width), half),
        in_specs=[in_vmem] * 2,
        out_specs=in_vmem,
        scratch_shapes=[
            pltpu.VMEM((depth, width), half),
            pltpu.VMEM((members, rows_here, depth), half),
            pltpu.VMEM((members, HALVES, half_rows, 2 * width), half),
            pltpu.VMEM((members, HALVES, members - 1, piece, 2 * width), half),
            pltpu.VMEM((members, HALVES, piece, 2 * width), half),
            dma((2,)),
            dma((members, HALVES)),
            dma((members, HALVES)),
            dma((members, HALVES)),
            dma((members, HALVES, members - 1)),
            dma((members, HALVES, members - 1)),
            dma((members, HALVES)),
            dma((HALVES, members)),
        ],
        compiler_params=pltpu.CompilerParams(
            collective_id=1, has_side_effects=True, vmem_limit_bytes=VMEM_BYTES
        ),
        name="project",
    )(attended, out_weight)


def solution(mesh):
    in_specs = (
        P("blk", "head"),
        P("blk", "head"),
        P("blk", "head"),
        P("blk", "head"),
        P("blk", "head"),
        P("head", "blk"),
        P(),
        P(),
        P(),
    )
    out_specs = P("blk", "head")
    return jax.shard_map(shards, mesh=mesh, in_specs=in_specs, out_specs=out_specs, check_vma=False)
```

```python
import functools

import jax
import jax.numpy as jnp
from jax import lax
from jax.experimental import pallas as pl
from jax.experimental.pallas import tpu as pltpu
from jax.sharding import PartitionSpec as P

HD = 128
BLOCK = 128
HOPS = 3
PIECES = 4
MIN_ROWS = 16
MESH = pl.DeviceIdType.MESH
VMEM_BYTES = 56 * 1024 * 1024
LOG2E = 1.4426950408889634


def collect(devices, k_ref, v_ref, k_all, v_all, own_sem, send_sem, recv_sem):
    me, row = lax.axis_index("blk"), lax.axis_index("head")
    left, right = lax.rem(me + devices - 1, devices), lax.rem(me + 1, devices)
    barrier = pltpu.get_barrier_semaphore()
    for other in (left, right):
        pl.semaphore_signal(barrier, inc=1, device_id=(other, row), device_id_type=MESH)
    pl.semaphore_wait(barrier, 2)
    size = k_ref.shape[0] // PIECES

    def hop(step, which, piece):
        source, store = ((k_ref, k_all), (v_ref, v_all))[which]
        rows = pl.ds(piece * size, size)
        return pltpu.make_async_remote_copy(
            src_ref=source.at[rows] if step == 0 else store.at[step, rows],
            dst_ref=store.at[step + 1, rows],
            send_sem=send_sem.at[step, which, piece],
            recv_sem=recv_sem.at[step, which, piece],
            device_id=(left, row),
            device_id_type=MESH,
        )

    parts = [(which, piece) for piece in range(PIECES) for which in range(2)]
    for part in parts:
        hop(0, *part).start()
    own = [
        pltpu.make_async_copy(k_ref, k_all.at[0], own_sem.at[0]),
        pltpu.make_async_copy(v_ref, v_all.at[0], own_sem.at[1]),
    ]
    for copy in own:
        copy.start()
    for step in range(1, HOPS):
        for part in parts:
            hop(step - 1, *part).wait_recv()
            hop(step, *part).start()
    for part in parts:
        hop(HOPS - 1, *part).wait_recv()
    for step in range(HOPS):
        for part in parts:
            hop(step, *part).wait_send()
    for copy in own:
        copy.wait()


def attend(
    devices, kvb, qdoc_ref, bdoc_ref, visit_ref, q_ref, k_ref, v_ref, rk_ref, rv_ref, o_ref,
    chosen, turned, top, total, acc
):
    me = lax.axis_index("blk")
    block_here = pl.program_id(1)
    row_blocks = pl.num_programs(1)
    query_block = me * row_blocks + block_here
    doc = qdoc_ref[query_block]
    slots = (HOPS + 1) * kvb

    def choose(slot, count):
        step = lax.div(slot, kvb)
        holder = lax.rem(me + step, devices)
        seen = visit_ref[query_block * slots + slot] == 1
        same = bdoc_ref[holder * kvb + lax.rem(slot, kvb)] == doc
        chosen[count] = slot
        return count + jnp.where(seen & same, 1, 0)

    chosen[0] = 0
    count = lax.fori_loop(0, slots, choose, 0)
    group = q_ref.shape[1] // HD
    for j in range(group):
        turned[:, j * BLOCK : (j + 1) * BLOCK] = q_ref[:, j * HD : (j + 1) * HD].T
    scale = HD**-0.5 * LOG2E

    def scored(keys):
        return jnp.dot(keys, turned[...], preferred_element_type=jnp.float32) * scale

    def weighted(values, weights):
        return lax.dot_general(
            values,
            weights.astype(jnp.bfloat16),
            (((0,), (0,)), ((), ())),
            preferred_element_type=jnp.float32,
        )

    scores = scored(rk_ref[...])
    place = lax.rem(lax.broadcasted_iota(jnp.int32, scores.shape, 1), BLOCK) + block_here * BLOCK
    scores = jnp.where(lax.broadcasted_iota(jnp.int32, scores.shape, 0) <= place, scores, -jnp.inf)
    first = jnp.max(scores, axis=0, keepdims=True)
    weights = jnp.exp2(scores - first)
    top[...] = first
    total[...] = jnp.sum(weights, axis=0, keepdims=True)
    acc[...] = weighted(rv_ref[...], weights)

    def add(keys, values):
        scores = scored(keys)
        before = top[...]
        now = jnp.maximum(before, jnp.max(scores, axis=0, keepdims=True))
        weights = jnp.exp2(scores - now)
        factor = jnp.exp2(before - now)
        top[...] = now
        total[...] = total[...] * factor + jnp.sum(weights, axis=0, keepdims=True)
        acc[...] = acc[...] * factor + weighted(values, weights)

    def rows_of(i):
        return pl.ds(pl.multiple_of(chosen[i] * BLOCK, BLOCK), BLOCK)

    def pair(i, carry):
        one, two = rows_of(2 * i), rows_of(2 * i + 1)
        add(
            jnp.concatenate([k_ref[one, :], k_ref[two, :]], axis=0),
            jnp.concatenate([v_ref[one, :], v_ref[two, :]], axis=0),
        )
        return carry

    lax.fori_loop(0, lax.div(count, 2), pair, 0)

    @pl.when(lax.rem(count, 2) == 1)
    def _():
        last = rows_of(count - 1)
        add(k_ref[last, :], v_ref[last, :])

    result = (acc[...] / total[...]).astype(jnp.bfloat16)
    for j in range(group):
        o_ref[:, j * HD : (j + 1) * HD] = result[:, j * BLOCK : (j + 1) * BLOCK].T


def project(
    members, a_ref, w_ref, out_ref, w_own, w_pair, blocks, parts, inbox, sums,
    w_sem, a_down, a_up, a_recv, part_send, part_recv, sum_send, sum_recv
):
    me, head = lax.axis_index("blk"), lax.axis_index("head")
    spot, core = lax.div(me, 2), lax.rem(me, 2)
    chunks, piece = sums.shape[1:3]
    half_rows = piece * members
    width = w_ref.shape[1]
    load = pltpu.make_async_copy(w_ref, w_own, w_sem.at[2])
    load.start()

    barrier = pltpu.get_barrier_semaphore()
    for p in range(members):
        for h in range(members):
            @pl.when((p != spot) | (h != head))
            def _():
                pl.semaphore_signal(
                    barrier, inc=1, device_id=(2 * p + core, h), device_id_type=MESH
                )
    pl.semaphore_signal(barrier, inc=1, device_id=(2 * spot + 1 - core, head), device_id_type=MESH)
    pl.semaphore_wait(barrier, members * members)

    def along(source, half, down):
        rows = pl.ds(half * half_rows, half_rows)
        return functools.partial(
            pltpu.make_async_remote_copy,
            dst_ref=blocks.at[source, rows],
            send_sem=(a_down if down else a_up).at[source, half],
            recv_sem=a_recv.at[source, half],
            device_id=(2 * (spot - 1 if down else spot + 1) + core, head),
            device_id_type=MESH,
        )

    def pass_on(source, half, own, down, act):
        rows = pl.ds(half * half_rows, half_rows)
        origin = a_ref.at[rows] if own else blocks.at[source, rows]

        @pl.when(spot > 0 if down else spot < members - 1)
        def _():
            act(along(source, half, down)(src_ref=origin))

    start = lambda copy: copy.start()
    finish = lambda copy: copy.wait_send()
    for half in range(chunks):
        pass_on(spot, half, True, True, start)
        pass_on(spot, half, True, False, start)
    swap = pltpu.make_async_remote_copy(
        src_ref=w_ref,
        dst_ref=w_pair,
        send_sem=w_sem.at[0],
        recv_sem=w_sem.at[1],
        device_id=(2 * spot + 1 - core, head),
        device_id_type=MESH,
    )
    swap.start()

    def part_copy(source, half, k):
        peer = lax.rem(head + k, members)
        return pltpu.make_async_remote_copy(
            src_ref=parts.at[source, half, pl.ds(pl.multiple_of(peer * piece, piece), piece)],
            dst_ref=inbox.at[source, half, k - 1],
            send_sem=part_send.at[source, half, k - 1],
            recv_sem=part_recv.at[source, half, k - 1],
            device_id=(me, peer),
            device_id_type=MESH,
        )

    def sum_copy(source, half):
        rows = pl.ds(pl.multiple_of(half * half_rows + head * piece, piece), piece)
        return pltpu.make_async_remote_copy(
            src_ref=sums.at[source, half],
            dst_ref=out_ref.at[rows],
            send_sem=sum_send.at[source, half],
            recv_sem=sum_recv.at[half, head],
            device_id=(2 * source + core, spot),
            device_id_type=MESH,
        )

    def multiply(source, half, own):
        rows = pl.ds(half * half_rows, half_rows)
        left = a_ref.at[rows] if own else blocks.at[source, rows]
        tile = min(width, 512)
        for right, place in ((w_own, core), (w_pair, 1 - core)):
            if own and half == 0:
                if right is w_pair:
                    swap.wait_recv()
                else:
                    load.wait()

            @pl.loop(0, width // tile)
            def _(t):
                at = pl.multiple_of(t * tile, tile)
                to = pl.multiple_of(place * width + t * tile, tile)
                parts[source, half, :, pl.ds(to, tile)] = jnp.dot(
                    left[...], right[:, pl.ds(at, tile)], preferred_element_type=jnp.float32
                ).astype(jnp.bfloat16)

    def spread(source, half, own, from_above):
        if not own:
            along(source, half, from_above)(src_ref=blocks.at[source, pl.ds(half * half_rows, half_rows)]).wait_recv()
            pass_on(source, half, False, from_above, start)
        multiply(source, half, own)
        for k in range(1, members):
            part_copy(source, half, k).start()

    def reduce(source, half):
        mine = pl.ds(pl.multiple_of(head * piece, piece), piece)
        value = parts[source, half, mine, :].astype(jnp.float32)
        for k in range(1, members):
            part_copy(source, half, k).wait_recv()
            value += inbox[source, half, k - 1].astype(jnp.float32)
        here = (source == spot) & (head == spot)
        rows = pl.ds(pl.multiple_of(half * half_rows + head * piece, piece), piece)

        @pl.when(here)
        def _():
            out_ref[rows, :] = value.astype(jnp.bfloat16)

        @pl.when(jnp.logical_not(here))
        def _():
            sums[source, half] = value.astype(jnp.bfloat16)
            sum_copy(source, half).start()

    events = [(spot, half, True, False, None) for half in range(chunks)]
    for step in range(1, members):
        for half in range(chunks):
            events.append((spot + step, half, False, True, spot + step < members))
            events.append((spot - step, half, False, False, spot - step >= 0))

    def run(valid, work):
        if valid is None:
            work()
        else:
            pl.when(valid)(work)

    lag = 2
    for i in range(len(events) + lag):
        if i < len(events):
            source, half, own, from_above, valid = events[i]
            run(valid, functools.partial(spread, source, half, own, from_above))
        if i >= lag:
            source, half, _, _, valid = events[i - lag]
            run(valid, functools.partial(reduce, source, half))

    for source, half, own, from_above, valid in events:
        def done(source=source, half=half, own=own, from_above=from_above):
            if own:
                pass_on(source, half, True, True, finish)
                pass_on(source, half, True, False, finish)
            else:
                pass_on(source, half, False, from_above, finish)
            for k in range(1, members):
                part_copy(source, half, k).wait_send()

            @pl.when((source != spot) | (head != spot))
            def _():
                sum_copy(source, half).wait_send()

        run(valid, done)
    swap.wait_send()
    for half in range(chunks):
        for k in range(members):
            rows = pl.ds(half * half_rows + k * piece, piece)

            @pl.when((k != head) | (spot != head))
            def _():
                pltpu.make_async_remote_copy(
                    src_ref=sums.at[0, 0],
                    dst_ref=out_ref.at[rows],
                    send_sem=sum_send.at[0, 0],
                    recv_sem=sum_recv.at[half, k],
                    device_id=(2 * head + core, k),
                    device_id_type=MESH,
                ).wait_recv()


def shards(
    queries,
    context_keys,
    context_values,
    response_keys,
    response_values,
    out_weight,
    query_docs,
    block_docs,
    visits,
):
    devices, members = lax.axis_size("blk"), lax.axis_size("head")
    assert devices == 2 * members
    rows_here, lanes = queries.shape
    key_rows, key_lanes = context_keys.shape
    heads_here = key_lanes // HD
    group = lanes // heads_here
    kvb = key_rows // BLOCK
    slots = HOPS + 1
    dma = pltpu.SemaphoreType.DMA
    anywhere = pl.BlockSpec(memory_space=pl.ANY)
    in_vmem = pl.BlockSpec(memory_space=pltpu.VMEM)
    in_smem = pl.BlockSpec(memory_space=pltpu.SMEM)

    store = jax.ShapeDtypeStruct((slots, key_rows, key_lanes), jnp.bfloat16)
    all_keys, all_values = pl.pallas_call(
        functools.partial(collect, devices),
        out_shape=(store, store),
        in_specs=[anywhere] * 2,
        out_specs=(anywhere, anywhere),
        scratch_shapes=[dma((2,)), dma((HOPS, 2, PIECES)), dma((HOPS, 2, PIECES))],
        compiler_params=pltpu.CompilerParams(
            collective_id=0, has_side_effects=True, vmem_limit_bytes=VMEM_BYTES
        ),
        name="collect",
    )(context_keys, context_values)

    whole = lambda: pl.BlockSpec((slots * key_rows, HD), lambda g, b: (0, g))
    own = lambda: pl.BlockSpec((rows_here, HD), lambda g, b: (0, g))
    attended = pl.pallas_call(
        functools.partial(attend, devices, kvb),
        grid=(heads_here, rows_here // BLOCK),
        out_shape=jax.ShapeDtypeStruct((rows_here, lanes), jnp.bfloat16),
        in_specs=[in_smem] * 3
        + [pl.BlockSpec((BLOCK, group), lambda g, b: (b, g)), whole(), whole(), own(), own()],
        out_specs=pl.BlockSpec((BLOCK, group), lambda g, b: (b, g)),
        scratch_shapes=[
            pltpu.SMEM((slots * kvb + 1,), jnp.int32),
            pltpu.VMEM((HD, group // HD * BLOCK), jnp.bfloat16),
            pltpu.VMEM((1, group // HD * BLOCK), jnp.float32),
            pltpu.VMEM((1, group // HD * BLOCK), jnp.float32),
            pltpu.VMEM((HD, group // HD * BLOCK), jnp.float32),
        ],
        compiler_params=pltpu.CompilerParams(vmem_limit_bytes=VMEM_BYTES),
        name="attend",
    )(
        query_docs,
        block_docs,
        visits.reshape(-1),
        queries,
        all_keys.reshape(slots * key_rows, key_lanes),
        all_values.reshape(slots * key_rows, key_lanes),
        response_keys,
        response_values,
    )

    depth, width = out_weight.shape
    chunks = rows_here // (MIN_ROWS * members)
    half_rows = rows_here // chunks
    piece = half_rows // members
    half = jnp.bfloat16
    return pl.pallas_call(
        functools.partial(project, members),
        out_shape=jax.ShapeDtypeStruct((rows_here, 2 * width), half),
        in_specs=[in_vmem, anywhere],
        out_specs=in_vmem,
        scratch_shapes=[
            pltpu.VMEM((depth, width), half),
            pltpu.VMEM((depth, width), half),
            pltpu.VMEM((members, rows_here, depth), half),
            pltpu.VMEM((members, chunks, half_rows, 2 * width), half),
            pltpu.VMEM((members, chunks, members - 1, piece, 2 * width), half),
            pltpu.VMEM((members, chunks, piece, 2 * width), half),
            dma((3,)),
            dma((members, chunks)),
            dma((members, chunks)),
            dma((members, chunks)),
            dma((members, chunks, members - 1)),
            dma((members, chunks, members - 1)),
            dma((members, chunks)),
            dma((chunks, members)),
        ],
        compiler_params=pltpu.CompilerParams(
            collective_id=1, has_side_effects=True, vmem_limit_bytes=VMEM_BYTES
        ),
        name="project",
    )(attended, out_weight)


def solution(mesh):
    in_specs = (
        P("blk", "head"),
        P("blk", "head"),
        P("blk", "head"),
        P("blk", "head"),
        P("blk", "head"),
        P("head", "blk"),
        P(),
        P(),
        P(),
    )
    out_specs = P("blk", "head")
    return jax.shard_map(shards, mesh=mesh, in_specs=in_specs, out_specs=out_specs, check_vma=False)
```

```python
import functools

import jax
import jax.numpy as jnp
from jax import lax
from jax.experimental import pallas as pl
from jax.experimental.pallas import tpu as pltpu
from jax.sharding import PartitionSpec as P

HD = 128
BLOCK = 128
HOPS = 3
PIECES = 4
MIN_ROWS = 16
MESH = pl.DeviceIdType.MESH
VMEM_BYTES = 56 * 1024 * 1024
LOG2E = 1.4426950408889634


def collect(devices, k_ref, v_ref, k_all, v_all, own_sem, send_sem, recv_sem):
    me, row = lax.axis_index("blk"), lax.axis_index("head")
    left, right = lax.rem(me + devices - 1, devices), lax.rem(me + 1, devices)
    barrier = pltpu.get_barrier_semaphore()
    for other in (left, right):
        pl.semaphore_signal(barrier, inc=1, device_id=(other, row), device_id_type=MESH)
    pl.semaphore_wait(barrier, 2)
    size = k_ref.shape[0] // PIECES

    def hop(step, which, piece):
        source, store = ((k_ref, k_all), (v_ref, v_all))[which]
        rows = pl.ds(piece * size, size)
        return pltpu.make_async_remote_copy(
            src_ref=source.at[rows] if step == 0 else store.at[step, rows],
            dst_ref=store.at[step + 1, rows],
            send_sem=send_sem.at[step, which, piece],
            recv_sem=recv_sem.at[step, which, piece],
            device_id=(left, row),
            device_id_type=MESH,
        )

    parts = [(which, piece) for piece in range(PIECES) for which in range(2)]
    for part in parts:
        hop(0, *part).start()
    own = [
        pltpu.make_async_copy(k_ref, k_all.at[0], own_sem.at[0]),
        pltpu.make_async_copy(v_ref, v_all.at[0], own_sem.at[1]),
    ]
    for copy in own:
        copy.start()
    for step in range(1, HOPS):
        for part in parts:
            hop(step - 1, *part).wait_recv()
            hop(step, *part).start()
    for part in parts:
        hop(HOPS - 1, *part).wait_recv()
    for step in range(HOPS):
        for part in parts:
            hop(step, *part).wait_send()
    for copy in own:
        copy.wait()


def attend(
    devices, kvb, qdoc_ref, bdoc_ref, visit_ref, q_ref, k_ref, v_ref, rk_ref, rv_ref, o_ref,
    chosen, turned, top, total, acc
):
    me = lax.axis_index("blk")
    block_here = pl.program_id(1)
    row_blocks = pl.num_programs(1)
    query_block = me * row_blocks + block_here
    doc = qdoc_ref[query_block]
    slots = (HOPS + 1) * kvb

    def choose(slot, count):
        step = lax.div(slot, kvb)
        holder = lax.rem(me + step, devices)
        seen = visit_ref[query_block * slots + slot] == 1
        same = bdoc_ref[holder * kvb + lax.rem(slot, kvb)] == doc
        chosen[count] = slot
        return count + jnp.where(seen & same, 1, 0)

    chosen[0] = 0
    count = lax.fori_loop(0, slots, choose, 0)
    group = q_ref.shape[1] // HD
    for j in range(group):
        turned[:, j * BLOCK : (j + 1) * BLOCK] = q_ref[:, j * HD : (j + 1) * HD].T
    scale = HD**-0.5 * LOG2E

    def scored(keys):
        return jnp.dot(keys, turned[...], preferred_element_type=jnp.float32) * scale

    def weighted(values, weights):
        return lax.dot_general(
            values,
            weights.astype(jnp.bfloat16),
            (((0,), (0,)), ((), ())),
            preferred_element_type=jnp.float32,
        )

    scores = scored(rk_ref[...])
    place = lax.rem(lax.broadcasted_iota(jnp.int32, scores.shape, 1), BLOCK) + block_here * BLOCK
    scores = jnp.where(lax.broadcasted_iota(jnp.int32, scores.shape, 0) <= place, scores, -jnp.inf)
    first = jnp.max(scores, axis=0, keepdims=True)
    weights = jnp.exp2(scores - first)
    top[...] = first
    total[...] = jnp.sum(weights, axis=0, keepdims=True)
    acc[...] = weighted(rv_ref[...], weights)

    def add(keys, values):
        scores = scored(keys)
        before = top[...]
        now = jnp.maximum(before, jnp.max(scores, axis=0, keepdims=True))
        weights = jnp.exp2(scores - now)
        factor = jnp.exp2(before - now)
        top[...] = now
        total[...] = total[...] * factor + jnp.sum(weights, axis=0, keepdims=True)
        acc[...] = acc[...] * factor + weighted(values, weights)

    def rows_of(i):
        return pl.ds(pl.multiple_of(chosen[i] * BLOCK, BLOCK), BLOCK)

    def pair(i, carry):
        one, two = rows_of(2 * i), rows_of(2 * i + 1)
        add(
            jnp.concatenate([k_ref[one, :], k_ref[two, :]], axis=0),
            jnp.concatenate([v_ref[one, :], v_ref[two, :]], axis=0),
        )
        return carry

    lax.fori_loop(0, lax.div(count, 2), pair, 0)

    @pl.when(lax.rem(count, 2) == 1)
    def _():
        last = rows_of(count - 1)
        add(k_ref[last, :], v_ref[last, :])

    result = (acc[...] / total[...]).astype(jnp.bfloat16)
    for j in range(group):
        o_ref[:, j * HD : (j + 1) * HD] = result[:, j * BLOCK : (j + 1) * BLOCK].T


def project(
    members, a_ref, w_ref, out_ref, w_own, w_pair, blocks, parts, inbox, sums,
    w_sem, a_down, a_up, a_recv, part_send, part_recv, sum_send, sum_recv
):
    me, head = lax.axis_index("blk"), lax.axis_index("head")
    spot, core = lax.div(me, 2), lax.rem(me, 2)
    chunks, piece = sums.shape[1:3]
    half_rows = piece * members
    width = w_ref.shape[1]
    load = pltpu.make_async_copy(w_ref, w_own, w_sem.at[2])
    load.start()

    barrier = pltpu.get_barrier_semaphore()
    for p in range(members):
        for h in range(members):
            @pl.when((p != spot) | (h != head))
            def _():
                pl.semaphore_signal(
                    barrier, inc=1, device_id=(2 * p + core, h), device_id_type=MESH
                )
    pl.semaphore_signal(barrier, inc=1, device_id=(2 * spot + 1 - core, head), device_id_type=MESH)
    pl.semaphore_wait(barrier, members * members)

    def along(source, half, down):
        rows = pl.ds(half * half_rows, half_rows)
        return functools.partial(
            pltpu.make_async_remote_copy,
            dst_ref=blocks.at[source, rows],
            send_sem=(a_down if down else a_up).at[source, half],
            recv_sem=a_recv.at[source, half],
            device_id=(2 * (spot - 1 if down else spot + 1) + core, head),
            device_id_type=MESH,
        )

    def pass_on(source, half, own, down, act):
        rows = pl.ds(half * half_rows, half_rows)
        origin = a_ref.at[rows] if own else blocks.at[source, rows]

        @pl.when(spot > 0 if down else spot < members - 1)
        def _():
            act(along(source, half, down)(src_ref=origin))

    start = lambda copy: copy.start()
    finish = lambda copy: copy.wait_send()
    for half in range(chunks):
        pass_on(spot, half, True, True, start)
        pass_on(spot, half, True, False, start)
    swap = pltpu.make_async_remote_copy(
        src_ref=w_ref,
        dst_ref=w_pair,
        send_sem=w_sem.at[0],
        recv_sem=w_sem.at[1],
        device_id=(2 * spot + 1 - core, head),
        device_id_type=MESH,
    )
    swap.start()

    def part_copy(source, half, k):
        peer = lax.rem(head + k, members)
        return pltpu.make_async_remote_copy(
            src_ref=parts.at[source, half, pl.ds(pl.multiple_of(peer * piece, piece), piece)],
            dst_ref=inbox.at[source, half, k - 1],
            send_sem=part_send.at[source, half, k - 1],
            recv_sem=part_recv.at[source, half, k - 1],
            device_id=(me, peer),
            device_id_type=MESH,
        )

    def sum_copy(source, half):
        rows = pl.ds(pl.multiple_of(half * half_rows + head * piece, piece), piece)
        return pltpu.make_async_remote_copy(
            src_ref=sums.at[source, half],
            dst_ref=out_ref.at[rows],
            send_sem=sum_send.at[source, half],
            recv_sem=sum_recv.at[half, head],
            device_id=(2 * source + core, spot),
            device_id_type=MESH,
        )

    def multiply(source, half, own):
        rows = pl.ds(half * half_rows, half_rows)
        left = a_ref.at[rows] if own else blocks.at[source, rows]
        tile = min(width, 512)
        for right, place in ((w_own, core), (w_pair, 1 - core)):
            if own and half == 0:
                if right is w_pair:
                    swap.wait_recv()
                else:
                    load.wait()

            @pl.loop(0, width // tile)
            def _(t):
                at = pl.multiple_of(t * tile, tile)
                to = pl.multiple_of(place * width + t * tile, tile)
                parts[source, half, :, pl.ds(to, tile)] = jnp.dot(
                    left[...], right[:, pl.ds(at, tile)], preferred_element_type=jnp.float32
                ).astype(jnp.bfloat16)

    def spread(source, half, own, from_above):
        if not own:
            along(source, half, from_above)(src_ref=blocks.at[source, pl.ds(half * half_rows, half_rows)]).wait_recv()
            pass_on(source, half, False, from_above, start)
        multiply(source, half, own)
        for k in range(1, members):
            part_copy(source, half, k).start()

    def reduce(source, half):
        mine = pl.ds(pl.multiple_of(head * piece, piece), piece)
        value = parts[source, half, mine, :].astype(jnp.float32)
        for k in range(1, members):
            part_copy(source, half, k).wait_recv()
            value += inbox[source, half, k - 1].astype(jnp.float32)
        here = (source == spot) & (head == spot)
        rows = pl.ds(pl.multiple_of(half * half_rows + head * piece, piece), piece)

        @pl.when(here)
        def _():
            out_ref[rows, :] = value.astype(jnp.bfloat16)

        @pl.when(jnp.logical_not(here))
        def _():
            sums[source, half] = value.astype(jnp.bfloat16)
            sum_copy(source, half).start()

    events = [(spot, half, True, False, None) for half in range(chunks)]
    for step in range(1, members):
        for half in range(chunks):
            events.append((spot + step, half, False, True, spot + step < members))
            events.append((spot - step, half, False, False, spot - step >= 0))

    def run(valid, work):
        if valid is None:
            work()
        else:
            pl.when(valid)(work)

    lag = 2
    for i in range(len(events) + lag):
        if i < len(events):
            source, half, own, from_above, valid = events[i]
            run(valid, functools.partial(spread, source, half, own, from_above))
        if i >= lag:
            source, half, own, _, valid = events[i - lag]
            soon = None if own else valid & (source > 0) & (source < members - 1)
            run(soon, functools.partial(reduce, source, half))

    for source, half, own, from_above, valid in events:
        def sent(source=source, half=half, own=own, from_above=from_above):
            if own:
                pass_on(source, half, True, True, finish)
                pass_on(source, half, True, False, finish)
            else:
                pass_on(source, half, False, from_above, finish)

        run(valid, sent)
    for source, half, own, _, valid in events:
        if not own:
            late = valid & ((source == 0) | (source == members - 1))
            run(late, functools.partial(reduce, source, half))

    for source, half, own, from_above, valid in events:
        def done(source=source, half=half):
            for k in range(1, members):
                part_copy(source, half, k).wait_send()

            @pl.when((source != spot) | (head != spot))
            def _():
                sum_copy(source, half).wait_send()

        run(valid, done)
    swap.wait_send()
    for half in range(chunks):
        for k in range(members):
            rows = pl.ds(half * half_rows + k * piece, piece)

            @pl.when((k != head) | (spot != head))
            def _():
                pltpu.make_async_remote_copy(
                    src_ref=sums.at[0, 0],
                    dst_ref=out_ref.at[rows],
                    send_sem=sum_send.at[0, 0],
                    recv_sem=sum_recv.at[half, k],
                    device_id=(2 * head + core, k),
                    device_id_type=MESH,
                ).wait_recv()


def shards(
    queries,
    context_keys,
    context_values,
    response_keys,
    response_values,
    out_weight,
    query_docs,
    block_docs,
    visits,
):
    devices, members = lax.axis_size("blk"), lax.axis_size("head")
    assert devices == 2 * members
    rows_here, lanes = queries.shape
    key_rows, key_lanes = context_keys.shape
    heads_here = key_lanes // HD
    group = lanes // heads_here
    kvb = key_rows // BLOCK
    slots = HOPS + 1
    dma = pltpu.SemaphoreType.DMA
    anywhere = pl.BlockSpec(memory_space=pl.ANY)
    in_vmem = pl.BlockSpec(memory_space=pltpu.VMEM)
    in_smem = pl.BlockSpec(memory_space=pltpu.SMEM)

    store = jax.ShapeDtypeStruct((slots, key_rows, key_lanes), jnp.bfloat16)
    all_keys, all_values = pl.pallas_call(
        functools.partial(collect, devices),
        out_shape=(store, store),
        in_specs=[anywhere] * 2,
        out_specs=(anywhere, anywhere),
        scratch_shapes=[dma((2,)), dma((HOPS, 2, PIECES)), dma((HOPS, 2, PIECES))],
        compiler_params=pltpu.CompilerParams(
            collective_id=0, has_side_effects=True, vmem_limit_bytes=VMEM_BYTES
        ),
        name="collect",
    )(context_keys, context_values)

    whole = lambda: pl.BlockSpec((slots * key_rows, HD), lambda g, b: (0, g))
    own = lambda: pl.BlockSpec((rows_here, HD), lambda g, b: (0, g))
    attended = pl.pallas_call(
        functools.partial(attend, devices, kvb),
        grid=(heads_here, rows_here // BLOCK),
        out_shape=jax.ShapeDtypeStruct((rows_here, lanes), jnp.bfloat16),
        in_specs=[in_smem] * 3
        + [pl.BlockSpec((BLOCK, group), lambda g, b: (b, g)), whole(), whole(), own(), own()],
        out_specs=pl.BlockSpec((BLOCK, group), lambda g, b: (b, g)),
        scratch_shapes=[
            pltpu.SMEM((slots * kvb + 1,), jnp.int32),
            pltpu.VMEM((HD, group // HD * BLOCK), jnp.bfloat16),
            pltpu.VMEM((1, group // HD * BLOCK), jnp.float32),
            pltpu.VMEM((1, group // HD * BLOCK), jnp.float32),
            pltpu.VMEM((HD, group // HD * BLOCK), jnp.float32),
        ],
        compiler_params=pltpu.CompilerParams(vmem_limit_bytes=VMEM_BYTES),
        name="attend",
    )(
        query_docs,
        block_docs,
        visits.reshape(-1),
        queries,
        all_keys.reshape(slots * key_rows, key_lanes),
        all_values.reshape(slots * key_rows, key_lanes),
        response_keys,
        response_values,
    )

    depth, width = out_weight.shape
    chunks = rows_here // (MIN_ROWS * members)
    half_rows = rows_here // chunks
    piece = half_rows // members
    half = jnp.bfloat16
    return pl.pallas_call(
        functools.partial(project, members),
        out_shape=jax.ShapeDtypeStruct((rows_here, 2 * width), half),
        in_specs=[in_vmem, anywhere],
        out_specs=in_vmem,
        scratch_shapes=[
            pltpu.VMEM((depth, width), half),
            pltpu.VMEM((depth, width), half),
            pltpu.VMEM((members, rows_here, depth), half),
            pltpu.VMEM((members, chunks, half_rows, 2 * width), half),
            pltpu.VMEM((members, chunks, members - 1, piece, 2 * width), half),
            pltpu.VMEM((members, chunks, piece, 2 * width), half),
            dma((3,)),
            dma((members, chunks)),
            dma((members, chunks)),
            dma((members, chunks)),
            dma((members, chunks, members - 1)),
            dma((members, chunks, members - 1)),
            dma((members, chunks)),
            dma((chunks, members)),
        ],
        compiler_params=pltpu.CompilerParams(
            collective_id=1, has_side_effects=True, vmem_limit_bytes=VMEM_BYTES
        ),
        name="project",
    )(attended, out_weight)


def solution(mesh):
    in_specs = (
        P("blk", "head"),
        P("blk", "head"),
        P("blk", "head"),
        P("blk", "head"),
        P("blk", "head"),
        P("head", "blk"),
        P(),
        P(),
        P(),
    )
    out_specs = P("blk", "head")
    return jax.shard_map(shards, mesh=mesh, in_specs=in_specs, out_specs=out_specs, check_vma=False)
```
